512 devices in a mesh: ctx: 64 (over x, y_lo, z), kv: 8 (over y_hi, core).
Axes of the slice: x: 4, y: 8 (y_hi: 4, y_lo: 2; y = y_hi * 2 + y_lo), z: 8, core: 2. Of those that a mesh axis runs over, the one named last changes fastest.
Arguments:
- queries: bfloat16 [8192, 4096], P('ctx', 'kv'), may hold values from -6 to 6
- key_rows: bfloat16 [8192, 1024], P('ctx', 'kv'), may hold values from -6 to 6
- value_rows: bfloat16 [8192, 1024], P('ctx', 'kv'), may hold values from -6 to 6
- grad_out: bfloat16 [8192, 4096], P('ctx', 'kv'), may hold values from -6 to 6
- fwd_out: bfloat16 [8192, 4096], P('ctx', 'kv'), may hold values from -0.59765625 to 0.59765625
- log_norm: float32 [32, 8192], P('kv', 'ctx'), may hold values from 3 to 6
- span_order: int32 [128], P('ctx'), may hold values from 0 to 127, as said below
- doc_lengths: int32 [2], replicated, may hold values from 1 to 5120, 8192 in all
- key_proj: bfloat16 [4096, 1024], P(None, 'kv'), may hold values from -0.1875 to 0.1875
- value_proj: bfloat16 [4096, 1024], P(None, 'kv'), may hold values from -0.1875 to 0.1875
Outputs:
- grad_query: bfloat16 [8192, 4096], P('ctx', 'kv')
- grad_key: bfloat16 [8192, 1024], P('ctx', 'kv')
- grad_value: bfloat16 [8192, 1024], P('ctx', 'kv')
- grad_hidden: bfloat16 [8192, 4096], P('ctx', 'kv')
The draws below stay inside these ranges and needn't reach their ends.
Inputs may be any that keep to these rules, and one draw needn't show every extreme that they name: `span_order`: A permutation of the 128 spans in which slots 2i and 2i + 1 hold spans that sum to 127. `doc_lengths`: the two lengths sum to 8192; neither is more than 5120.
All inputs are finite; a program needn't handle non-finite values.
Results may differ from the reference program's by a relative error of at most 0.022.
Values may be sent and summed in bfloat16 or wider, within the bound.
No kernel may reach another device: no remote copies, remote signals or barrier semaphores. Data moves between devices by JAX's collectives and lax.ppermute only.
A program may use at most 64 MiB of HBM per device.

```python
import math
import jax
import jax.numpy as jnp
import numpy as np
from jax import lax

SPAN = 64
HD = 128
HQ = 4
DW = 4096
KV_HEADS = 8
SPANS = 128
SEQ = 8192
MOSTLEN = 5120


def draw_span_order(key, part):
    key = jax.random.fold_in(key, 11)
    half_count = SPANS // 2
    early = jax.random.permutation(key, half_count).astype(jnp.int32)
    late = (SPANS - 1 - early).astype(jnp.int32)
    flipped = jax.random.randint(jax.random.fold_in(key, 5), (half_count,), 0, 2).astype(jnp.int32)
    first_slot = jnp.where(flipped == 1, late, early)
    second_slot = jnp.where(flipped == 1, early, late)
    return jnp.stack([first_slot, second_slot], axis=1).reshape(SPANS).astype(jnp.int32)


def levels(stream_key, extent, split, smallest, largest):
    factor_of, own = 1.0, jax.random.fold_in(stream_key, 6)
    for position, blocks in split:
        heights = jnp.exp(jax.random.uniform(jax.random.fold_in(own, position), (blocks,), jnp.float32, smallest / len(split), largest / len(split)))
        factor_of = factor_of * jnp.repeat(heights, extent[position] // blocks).reshape([-1 if axis == position else 1 for axis in range(len(extent))])
    return factor_of


def split_up(count, total, most, lean):
    portions = [(1 << 20) // math.isqrt(rank ** lean) + 1 for rank in range(2, count + 1)]
    surplus, holding = total - most - (count - 1), [1] * (count - 1)
    while surplus > 0:
        free = [i for i in range(count - 1) if holding[i] < most]
        pool, budget = sum([portions[i] for i in free]), surplus
        for i in free:
            addition = min(most - holding[i], max(1, budget * portions[i] // pool), surplus)
            holding[i] = holding[i] + addition
            surplus = surplus - addition
    return np.array([most] + holding)


def ragged(stream_key, number_of, total, reach, slope):
    if number_of == 2:
        one = jax.random.randint(stream_key, (), max(1, total - reach), min(reach, total - 1) + 1)
        return jnp.stack([one, total - one])
    lengths = jnp.asarray(split_up(number_of, total, reach, slope), jnp.int32)
    couples = (number_of - 1) // 2
    source_of, receiver = lengths[1:1 + 2 * couples:2], lengths[2:2 + 2 * couples:2]
    room = jnp.minimum(source_of - 1, reach - receiver)
    moved = jax.random.randint(jax.random.fold_in(stream_key, 1), (couples,), 0, 1 << 20) % (room + 1)
    lengths = lengths.at[1:1 + 2 * couples:2].set(source_of - moved).at[2:2 + 2 * couples:2].set(receiver + moved)
    return lengths[jax.random.permutation(jax.random.fold_in(stream_key, 2), number_of)]


def bell_draw(stream_key, dims, width, most, split=(), held_as=jnp.bfloat16):
    values = jax.random.normal(stream_key, dims, jnp.float32) * width
    if len(split) > 0:
        values = levels(stream_key, dims, split, -0.22, 0.18) * values
    return jnp.clip(values, min=-most, max=most).astype(held_as)


def setup_inputs(seed: int = 0) -> dict:
    key_list = jax.random.split(jax.random.key(seed), 11)
    return {
        "queries": bell_draw(key_list[0], (SEQ, KV_HEADS * HQ * HD), 1.0, 6.0, ((0, 64), (1, 8))),
        "key_rows": bell_draw(key_list[1], (SEQ, KV_HEADS * HD), 1.0, 6.0, ((0, 64), (1, 8))),
        "value_rows": bell_draw(key_list[2], (SEQ, KV_HEADS * HD), 1.0, 6.0, ((0, 64), (1, 8))),
        "grad_out": bell_draw(key_list[3], (SEQ, KV_HEADS * HQ * HD), 1.0, 6.0, ((0, 64), (1, 8))),
        "fwd_out": bell_draw(key_list[4], (SEQ, KV_HEADS * HQ * HD), 0.1, 0.59765625, ((0, 64), (1, 8))),
        "log_norm": jnp.clip(3.0 + 3.0 * jax.random.uniform(key_list[5], (KV_HEADS * HQ, SEQ), jnp.float32) ** levels(key_list[5], (KV_HEADS * HQ, SEQ), ((0, 8), (1, 64)), -0.2, 0.2), 3.0, 6.0),
        "span_order": draw_span_order(jax.random.fold_in(key_list[10], 71), 0),
        "doc_lengths": ragged(key_list[7], 2, SEQ, MOSTLEN, 0).astype(jnp.int32),
        "key_proj": bell_draw(key_list[8], (DW, KV_HEADS * HD), (KV_HEADS * HD) ** -0.5, 0.1875, ((1, 8),)),
        "value_proj": bell_draw(key_list[9], (DW, KV_HEADS * HD), (KV_HEADS * HD) ** -0.5, 0.1875, ((1, 8),)),
    }


def contract_rows(left, right):
    return lax.dot_general(left, right, (((1,), (1,)), ((), ())), preferred_element_type=jnp.float32)

def reference(queries, key_rows, value_rows, grad_out, fwd_out, log_norm, span_order, doc_lengths, key_proj, value_proj):
    score_scale = 1.0 / math.sqrt(HD)
    slot_index = jnp.arange(SEQ, dtype=jnp.int32)
    positions = (span_order[slot_index // SPAN] * SPAN + slot_index % SPAN).astype(jnp.int32)
    late_doc = positions >= doc_lengths[0]
    block_len = math.gcd(SEQ, 512)
    block_count = SEQ // block_len
    query_all = queries.reshape(SEQ, KV_HEADS, HQ, HD)
    grad_all = grad_out.reshape(SEQ, KV_HEADS, HQ, HD)
    out_all = fwd_out.reshape(SEQ, KV_HEADS, HQ, HD)

    def group(group_index):
        group_index = group_index.astype(jnp.int32)
        query_g = lax.dynamic_slice_in_dim(query_all, group_index, 1, 1)[:, 0]
        grad_g = lax.dynamic_slice_in_dim(grad_all, group_index, 1, 1)[:, 0]
        out_g = lax.dynamic_slice_in_dim(out_all, group_index, 1, 1)[:, 0]
        key_g = lax.dynamic_slice_in_dim(key_rows, group_index * HD, HD, 1).astype(jnp.float32)
        value_g = lax.dynamic_slice_in_dim(value_rows, group_index * HD, HD, 1).astype(jnp.float32)
        norm_g = lax.dynamic_slice_in_dim(log_norm, group_index * HQ, HQ, 0)
        delta_g = lax.optimization_barrier(jnp.sum(grad_g.astype(jnp.float32) * out_g.astype(jnp.float32), axis=2))

        def step(carried, block_index):
            start = (block_index * block_len).astype(jnp.int32)
            query_b = lax.dynamic_slice_in_dim(query_g, start, block_len, 0).astype(jnp.float32)
            grad_b = lax.dynamic_slice_in_dim(grad_g, start, block_len, 0).astype(jnp.float32)
            delta_b = lax.dynamic_slice_in_dim(delta_g, start, block_len, 0).T
            norm_b = lax.dynamic_slice_in_dim(norm_g, start, block_len, 1)
            pos_b = lax.dynamic_slice_in_dim(positions, start, block_len, 0)
            late_b = lax.dynamic_slice_in_dim(late_doc, start, block_len, 0)
            live_mask = (positions[None, :] <= pos_b[:, None]) & (late_doc[None, :] == late_b[:, None])
            score = jnp.einsum('qhd,kd->hqk', query_b, key_g) * score_scale
            prob = jnp.where(live_mask[None], jnp.exp(score - norm_b[:, :, None]), 0.0)
            dprob = jnp.einsum('qhd,kd->hqk', grad_b, value_g)
            dscore = prob * (dprob - delta_b[:, :, None])
            prob_b = lax.optimization_barrier(prob.astype(jnp.bfloat16)).astype(jnp.float32)
            dscore_b = lax.optimization_barrier(dscore.astype(jnp.bfloat16)).astype(jnp.float32)
            grad_qb = (jnp.einsum('hqk,kd->qhd', dscore_b, key_g) * score_scale).astype(jnp.bfloat16)
            key_acc = carried[0] + jnp.einsum('hqk,qhd->kd', dscore_b, query_b)
            value_acc = carried[1] + jnp.einsum('hqk,qhd->kd', prob_b, grad_b)
            return ((key_acc, value_acc), grad_qb)
        empty = jnp.zeros((SEQ, HD), jnp.float32)
        sums, grad_blocks = lax.scan(step, (empty, empty), jnp.arange(block_count, dtype=jnp.int32))
        grad_qg = grad_blocks.reshape(SEQ, HQ, HD)
        grad_kg = (sums[0] * score_scale).astype(jnp.bfloat16)
        grad_vg = sums[1].astype(jnp.bfloat16)
        return (grad_qg, grad_kg, grad_vg)
    grad_qs, grad_ks, grad_vs = lax.map(group, jnp.arange(KV_HEADS, dtype=jnp.int32))
    grad_query = jnp.transpose(grad_qs, (1, 0, 2, 3)).reshape(SEQ, KV_HEADS * HQ * HD)
    grad_key = jnp.transpose(grad_ks, (1, 0, 2)).reshape(SEQ, KV_HEADS * HD)
    grad_value = jnp.transpose(grad_vs, (1, 0, 2)).reshape(SEQ, KV_HEADS * HD)
    hidden_sum = contract_rows(grad_key, key_proj) + contract_rows(grad_value, value_proj)
    grad_hidden = hidden_sum.astype(jnp.bfloat16)
    return (grad_query, grad_key, grad_value, grad_hidden)
```

```python
import math

import jax
import jax.numpy as jnp
from jax import lax
from jax.experimental import pallas as pl
from jax.experimental.pallas import tpu as pltpu
from jax.sharding import Mesh, PartitionSpec as P

AXES = ("x", "y_lo", "z", "y_hi", "core")
CTX = ("x", "y_lo", "z")
KEYS = ("y_lo", "z")
KV = ("y_hi", "core")
SPAN = 64
HD = 128
HQ = 4
TOK = 2 * SPAN
QROWS = HQ * SPAN
CHUNK = 256
PER = CHUNK // SPAN
QBLOCK = 2 * HQ * TOK + 32
KBLOCK = 2 * TOK + 16
BF = jnp.bfloat16
F32 = jnp.float32


def nt(a, b):
    return lax.dot_general(a, b, (((1,), (1,)), ((), ())), preferred_element_type=F32)


def nn(a, b):
    return lax.dot_general(a, b, (((1,), (0,)), ((), ())), preferred_element_type=F32)


def prep_kernel(span_ref, q_ref, g_ref, o_ref, lse_ref, out_ref):
    lse_rows, delta_rows = [], []
    for s in range(2):
        rows = slice(s * SPAN, (s + 1) * SPAN)
        for pair in range(HQ // 2):
            prods = []
            for h in (2 * pair, 2 * pair + 1):
                cols = slice(h * HD, (h + 1) * HD)
                at = s * QROWS + h * SPAN
                g = g_ref[rows, cols]
                out_ref[at : at + SPAN, :] = q_ref[rows, cols]
                out_ref[HQ * TOK + at : HQ * TOK + at + SPAN, :] = g
                prods.append(g.astype(F32) * o_ref[rows, cols].astype(F32))
            both = jnp.concatenate(prods, axis=0)
            delta_rows.append(jnp.sum(both.T, axis=0, keepdims=True))
            lse_rows.append(
                jnp.concatenate(
                    [lse_ref[2 * pair : 2 * pair + 1, rows], lse_ref[2 * pair + 1 : 2 * pair + 2, rows]],
                    axis=1,
                )
            )
    parts = []
    for rows in (lse_rows, delta_rows):
        rest = jnp.concatenate(rows, axis=0)
        for _ in range(3):
            piece = rest.astype(BF).astype(F32)
            rest = rest - piece
            parts.append(piece)
    line = lax.broadcasted_iota(jnp.int32, (8, HD), 0)
    spans = jnp.where(line == 0, span_ref[0], span_ref[1]).astype(F32)
    parts.append(spans)
    out_ref[2 * HQ * TOK :, :] = jnp.concatenate(parts, axis=0).astype(BF)


def tile_kernel(n_q, n_k, table, gq_ref, gkv_ref, dq_ref, dkv_ref, k_s, v_s, kt_s, dk_acc, dv_acc, dqt_acc, lse_s, del_s):
    spans_k = 2 * n_k
    scale = 1.0 / math.sqrt(HD)

    def rank_of(j):
        return table[j]

    def sorted_span(j):
        return table[spans_k + j]

    def q_info(i, what):
        return table[2 * spans_k + 4 * i + what]

    boundary = table[2 * spans_k + 8 * n_q]
    dk_acc[...] = jnp.zeros_like(dk_acc)
    dv_acc[...] = jnp.zeros_like(dv_acc)
    for w in range(n_k):
        for s in range(2):
            to = pl.ds(pl.multiple_of(rank_of(2 * w + s) * SPAN, SPAN), SPAN)
            k_s[to, :] = gkv_ref[w, s * SPAN : (s + 1) * SPAN, :]
            v_s[to, :] = gkv_ref[w, TOK + s * SPAN : TOK + (s + 1) * SPAN, :]
    for c in range(spans_k // PER):
        rows = slice(c * CHUNK, (c + 1) * CHUNK)
        kt_s[c] = k_s[rows, :].T
    for x in range(n_q):
        extra = gq_ref[x, 2 * HQ * TOK : 2 * HQ * TOK + 24, :].astype(F32)
        lse = extra[0:4] + extra[4:8] + extra[8:12]
        dlt = extra[12:16] + extra[16:20] + extra[20:24]
        for s in range(2):
            i = 2 * x + s
            lse_s[i] = jnp.broadcast_to(jnp.concatenate([lse[2 * s : 2 * s + 1], lse[2 * s + 1 : 2 * s + 2]], axis=1), (8, QROWS))
            del_s[i] = jnp.broadcast_to(jnp.concatenate([dlt[2 * s : 2 * s + 1], dlt[2 * s + 1 : 2 * s + 2]], axis=1), (8, QROWS))

    key_line = lax.broadcasted_iota(jnp.int32, (SPAN, QROWS), 0)
    row_off = lax.broadcasted_iota(jnp.int32, (1, QROWS), 1) % SPAN

    def q_step(i, _):
        x, s = i // 2, i % 2
        at = pl.multiple_of(s * QROWS, QROWS)
        q = gq_ref[x, pl.ds(at, QROWS), :]
        g = gq_ref[x, pl.ds(HQ * TOK + at, QROWS), :]
        lse = lse_s[i][0:1]
        dlt = del_s[i][0:1]
        q_pos = q_info(i, 0) * SPAN + row_off
        q_start = jnp.where(q_pos >= boundary, boundary, 0)
        dqt_acc[...] = jnp.zeros_like(dqt_acc)

        def k_step(c, _):
            rows = pl.ds(pl.multiple_of(c * CHUNK, CHUNK), CHUNK)
            k = k_s[rows, :]
            score = nt(k, q)
            dprob = nt(v_s[rows, :], g)
            probs, dscores = [], []
            for j in range(PER):
                part = slice(j * SPAN, (j + 1) * SPAN)
                base = sorted_span(c * PER + j) * SPAN
                live = (key_line <= q_pos - base) & (key_line >= q_start - base)
                prob = jnp.where(live, jnp.exp(score[part] * scale - lse), 0.0)
                probs.append(prob.astype(BF))
                dscores.append((prob * (dprob[part] - dlt)).astype(BF))
            prob_b = jnp.concatenate(probs, axis=0)
            dscore_b = jnp.concatenate(dscores, axis=0)
            dv_acc[rows, :] += nn(prob_b, g)
            dk_acc[rows, :] += nn(dscore_b, q)
            dqt_acc[...] += nn(kt_s[c], dscore_b)
            return 0

        lax.fori_loop(q_info(i, 1), q_info(i, 2), k_step, 0)
        dq = (dqt_acc[...] * scale).T.astype(BF)
        to = pl.ds(pl.multiple_of(i * SPAN, SPAN), SPAN)
        for h in range(HQ):
            dq_ref[to, h * HD : (h + 1) * HD] = dq[h * SPAN : (h + 1) * SPAN]
        return 0

    lax.fori_loop(0, 2 * n_q, q_step, 0)
    for w in range(n_k):
        for s in range(2):
            at = pl.ds(pl.multiple_of(rank_of(2 * w + s) * SPAN, SPAN), SPAN)
            dkv_ref[w, s * SPAN : (s + 1) * SPAN, :] = dk_acc[at, :].astype(BF)
            dkv_ref[w, TOK + s * SPAN : TOK + (s + 1) * SPAN, :] = dv_acc[at, :].astype(BF)


VMEM = pl.BlockSpec(memory_space=pltpu.VMEM)
SMEM = pl.BlockSpec(memory_space=pltpu.SMEM)


def tile_grads(table, gq, gkv):
    n_q, n_k = gq.shape[0], gkv.shape[0]
    keys = n_k * TOK
    return pl.pallas_call(
        lambda *refs: tile_kernel(n_q, n_k, *refs),
        out_shape=(
            jax.ShapeDtypeStruct((n_q * TOK, HQ * HD), BF),
            jax.ShapeDtypeStruct((n_k, 2 * TOK, HD), BF),
        ),
        in_specs=[SMEM, VMEM, VMEM],
        out_specs=(VMEM, VMEM),
        scratch_shapes=[
            pltpu.VMEM((keys, HD), BF),
            pltpu.VMEM((keys, HD), BF),
            pltpu.VMEM((keys // CHUNK, HD, CHUNK), BF),
            pltpu.VMEM((keys, HD), F32),
            pltpu.VMEM((keys, HD), F32),
            pltpu.VMEM((HD, QROWS), F32),
            pltpu.VMEM((2 * n_q, 8, QROWS), F32),
            pltpu.VMEM((2 * n_q, 8, QROWS), F32),
        ],
        compiler_params=pltpu.CompilerParams(vmem_limit_bytes=32 * 1024 * 1024),
        cost_estimate=pl.CostEstimate(flops=5_000_000_000, bytes_accessed=4_000_000, transcendentals=2_000_000),
        name="tile_grads",
    )(table, gq, gkv)


def prep(span_order, queries, grad_out, fwd_out, log_norm):
    return pl.pallas_call(
        prep_kernel,
        out_shape=jax.ShapeDtypeStruct((QBLOCK, HD), BF),
        in_specs=[SMEM, VMEM, VMEM, VMEM, VMEM],
        out_specs=VMEM,
        name="prep",
    )(span_order, queries, grad_out, fwd_out, log_norm)


def body(queries, key_rows, value_rows, grad_out, fwd_out, log_norm, span_order, doc_lengths, key_proj, value_proj):
    n_q, n_k = lax.axis_size("x"), lax.axis_size(KEYS)
    n_hi = lax.axis_size("y_hi")
    scale = 1.0 / math.sqrt(HD)
    core = lax.axis_index("core")
    y_hi = lax.axis_index("y_hi")

    tag = jnp.broadcast_to(jnp.pad(span_order, (0, 14))[:, None], (16, HD)).astype(BF)
    mine = jnp.concatenate([key_rows, value_rows, tag], axis=0)
    gkv = lax.all_to_all(jnp.broadcast_to(mine[None], (n_k, KBLOCK, HD)), KEYS, 0, 0)
    gq = lax.all_gather(prep(span_order, queries, grad_out, fwd_out, log_norm), "x", axis=0)

    cols = key_proj.shape[0] // (2 * n_hi)
    projs = jnp.stack([key_proj, value_proj], axis=0).reshape(2, n_hi, 2, cols, HD)
    kept = lax.dynamic_index_in_dim(projs, core, 2, keepdims=False)
    given = lax.dynamic_index_in_dim(projs, 1 - core, 2, keepdims=False)
    swapped = lax.ppermute(given, "core", [(0, 1), (1, 0)])
    both = jnp.stack([kept, swapped], axis=1)
    pieces = [lax.dynamic_index_in_dim(both, y_hi, 2, keepdims=False)]
    for shift in range(1, n_hi):
        out = lax.dynamic_index_in_dim(both, (y_hi + shift) % n_hi, 2, keepdims=False)
        pieces.append(lax.ppermute(out, "y_hi", [(i, (i + shift) % n_hi) for i in range(n_hi)]))

    q_span = gq[:, 2 * HQ * TOK + 24 : 2 * HQ * TOK + 26, 0].reshape(2 * n_q).astype(jnp.int32)
    k_span = gkv[:, 2 * TOK : 2 * TOK + 2, 0].reshape(2 * n_k).astype(jnp.int32)
    boundary = doc_lengths[0]
    rank = jnp.sum((k_span[None, :] < k_span[:, None]).astype(jnp.int32), axis=1)
    slots = jnp.arange(2 * n_k, dtype=jnp.int32)
    in_order = jnp.sum(jnp.where(rank[None, :] == slots[:, None], k_span[None, :], 0), axis=1)
    first = jnp.where(q_span * SPAN >= boundary, boundary // SPAN, 0)
    below = jnp.sum((k_span[None, :] < first[:, None]).astype(jnp.int32), axis=1)
    upto = jnp.sum((k_span[None, :] <= q_span[:, None]).astype(jnp.int32), axis=1)
    info = jnp.stack([q_span, below // PER, (upto + PER - 1) // PER, q_span], axis=1).reshape(8 * n_q)
    table = jnp.concatenate([rank, in_order, info, doc_lengths])

    dq, dkv = tile_grads(table, gq, gkv)
    grad_query = lax.psum_scatter(dq, "x", scatter_dimension=0, tiled=True)
    parts = lax.all_to_all(dkv, KEYS, 0, 0)
    total = jnp.sum(parts.astype(F32), axis=0)
    grad_key = (total[:TOK] * scale).astype(BF)
    grad_value = total[TOK:].astype(BF)

    groups = lax.all_gather(jnp.concatenate([grad_key, grad_value], axis=1), KV, axis=0)
    hidden = jnp.zeros((TOK, cols), F32)
    for shift in range(n_hi):
        for far in range(2):
            source = ((y_hi - shift) % n_hi) * 2 + (core if far == 0 else 1 - core)
            block = lax.dynamic_index_in_dim(groups, source, 0, keepdims=False)
            piece = pieces[shift]
            own_first = piece[:, far]
            weight = jnp.concatenate([own_first[0], own_first[1]], axis=1)
            hidden = hidden + nt(block, weight)
    return grad_query, grad_key, grad_value, hidden.astype(BF)


def solution(mesh):
    fine = Mesh(mesh.devices.reshape(4, 2, 8, 4, 2), AXES)
    placed = (
        P(CTX, KV),
        P(CTX, KV),
        P(CTX, KV),
        P(CTX, KV),
        P(CTX, KV),
        P(KV, CTX),
        P(CTX),
        P(),
        P(None, KV),
        P(None, KV),
    )
    return jax.shard_map(
        body,
        mesh=fine,
        in_specs=placed,
        out_specs=(P(CTX, KV), P(CTX, KV), P(CTX, KV), P(CTX, KV)),
        check_vma=False,
    )
```

```python
import math

import jax
import jax.numpy as jnp
from jax import lax
from jax.experimental import pallas as pl
from jax.experimental.pallas import tpu as pltpu
from jax.sharding import Mesh, PartitionSpec as P

AXES = ("x", "y_lo", "z", "y_hi", "core")
CTX = ("x", "y_lo", "z")
KEYS = ("y_lo", "z")
KV = ("y_hi", "core")
SPAN = 64
HD = 128
HQ = 4
TOK = 2 * SPAN
QROWS = HQ * SPAN
CHUNK = 256
UNROLL = 4
PER = CHUNK // SPAN
QBLOCK = 2 * HQ * TOK + 32
KBLOCK = 2 * TOK + 16
BF = jnp.bfloat16
F32 = jnp.float32
VMEM = pl.BlockSpec(memory_space=pltpu.VMEM)
SMEM = pl.BlockSpec(memory_space=pltpu.SMEM)


def nt(a, b):
    return lax.dot_general(a, b, (((1,), (1,)), ((), ())), preferred_element_type=F32)


def nn(a, b):
    return lax.dot_general(a, b, (((1,), (0,)), ((), ())), preferred_element_type=F32)


def span_lines(span_ref, lines):
    line = lax.broadcasted_iota(jnp.int32, (lines, HD), 0)
    return jnp.where(line == 0, span_ref[0], span_ref[1]).astype(F32)


def pack_kernel(span_ref, k_ref, v_ref, out_ref):
    k, v, tag = k_ref[...], v_ref[...], span_lines(span_ref, KBLOCK - 2 * TOK).astype(BF)
    for w in range(out_ref.shape[0]):
        out_ref[w, :TOK, :] = k
        out_ref[w, TOK : 2 * TOK, :] = v
        out_ref[w, 2 * TOK :, :] = tag


def prep_kernel(span_ref, q_ref, g_ref, o_ref, lse_ref, out_ref):
    lse_rows, delta_rows = [], []
    for s in range(2):
        rows = slice(s * SPAN, (s + 1) * SPAN)
        for pair in range(HQ // 2):
            prods = []
            for h in (2 * pair, 2 * pair + 1):
                cols = slice(h * HD, (h + 1) * HD)
                at = s * QROWS + h * SPAN
                g = g_ref[rows, cols]
                out_ref[at : at + SPAN, :] = q_ref[rows, cols]
                out_ref[HQ * TOK + at : HQ * TOK + at + SPAN, :] = g
                prods.append(g.astype(F32) * o_ref[rows, cols].astype(F32))
            both = jnp.concatenate(prods, axis=0)
            delta_rows.append(jnp.sum(both.T, axis=0, keepdims=True))
            lse_rows.append(
                jnp.concatenate(
                    [lse_ref[2 * pair : 2 * pair + 1, rows], lse_ref[2 * pair + 1 : 2 * pair + 2, rows]],
                    axis=1,
                )
            )
    parts = []
    for rows in (lse_rows, delta_rows):
        rest = jnp.concatenate(rows, axis=0)
        for _ in range(3):
            piece = rest.astype(BF).astype(F32)
            rest = rest - piece
            parts.append(piece)
    parts.append(span_lines(span_ref, 8))
    out_ref[2 * HQ * TOK :, :] = jnp.concatenate(parts, axis=0).astype(BF)


def tile_kernel(n_q, n_k, table, *refs):
    q_refs, (gkv_ref,), refs = refs[:n_q], refs[n_q : n_q + 1], refs[n_q + 1 :]
    dq_refs, (dkv_ref,), refs = refs[:n_q], refs[n_q : n_q + 1], refs[n_q + 1 :]
    q_s, g_s, k_s, v_s, kt_s, dk_acc, dv_acc, dqt_acc, lse_s, del_s = refs
    spans_k, most = 2 * n_k, 2 * n_q * 2 * n_k // PER
    scale = 1.0 / math.sqrt(HD)
    log2e = 1.0 / math.log(2.0)
    boundary, n_tiles = table[2 * spans_k + 3 * most], table[2 * spans_k + 3 * most + 1]

    dk_acc[...] = jnp.zeros_like(dk_acc)
    dv_acc[...] = jnp.zeros_like(dv_acc)
    dqt_acc[...] = jnp.zeros_like(dqt_acc)
    for w in range(n_k):
        for s in range(2):
            to = pl.ds(pl.multiple_of(table[2 * w + s] * SPAN, SPAN), SPAN)
            k_s[to, :] = gkv_ref[w, s * SPAN : (s + 1) * SPAN, :]
            v_s[to, :] = gkv_ref[w, TOK + s * SPAN : TOK + (s + 1) * SPAN, :]
    for c in range(spans_k // PER):
        kt_s[c] = k_s[c * CHUNK : (c + 1) * CHUNK, :].T
    for x in range(n_q):
        q_s[x * 2 * QROWS : (x + 1) * 2 * QROWS, :] = q_refs[x][: HQ * TOK, :]
        g_s[x * 2 * QROWS : (x + 1) * 2 * QROWS, :] = q_refs[x][HQ * TOK : 2 * HQ * TOK, :]
        extra = q_refs[x][2 * HQ * TOK : 2 * HQ * TOK + 24, :].astype(F32)
        lse = (extra[0:4] + extra[4:8] + extra[8:12]) * log2e
        dlt = extra[12:16] + extra[16:20] + extra[20:24]
        for s in range(2):
            i = 2 * x + s
            lse_s[i] = jnp.broadcast_to(jnp.concatenate([lse[2 * s : 2 * s + 1], lse[2 * s + 1 : 2 * s + 2]], axis=1), (8, QROWS))
            del_s[i] = jnp.broadcast_to(jnp.concatenate([dlt[2 * s : 2 * s + 1], dlt[2 * s + 1 : 2 * s + 2]], axis=1), (8, QROWS))

    key_line = lax.broadcasted_iota(jnp.int32, (SPAN, QROWS), 0)
    row_off = lax.broadcasted_iota(jnp.int32, (1, QROWS), 1) % SPAN

    def open_tile(t):
        at = 2 * spans_k + 3 * t
        span, i, c = table[at], table[at + 1], table[at + 2]
        q_rows = pl.ds(pl.multiple_of(i * QROWS, QROWS), QROWS)
        k_rows = pl.ds(pl.multiple_of(c * CHUNK, CHUNK), CHUNK)
        score = nt(k_s[k_rows, :], q_s[q_rows, :])
        dprob = nt(v_s[k_rows, :], g_s[q_rows, :])
        lse, dlt = lse_s[i][0:1], del_s[i][0:1]
        q_pos = span * SPAN + row_off
        q_start = jnp.where(q_pos >= boundary, boundary, 0)
        probs, dscores = [], []
        for j in range(PER):
            part = slice(j * SPAN, (j + 1) * SPAN)
            base = table[spans_k + c * PER + j] * SPAN
            live = (key_line <= q_pos - base) & (key_line >= q_start - base)
            prob = jnp.where(live, jnp.exp2(score[part] * (scale * log2e) - lse), 0.0)
            probs.append(prob.astype(BF))
            dscores.append((prob * (dprob[part] - dlt)).astype(BF))
        return i, c, q_rows, k_rows, jnp.concatenate(probs, axis=0), jnp.concatenate(dscores, axis=0)

    def close_tile(i, c, q_rows, k_rows, prob_b, dscore_b):
        dv_acc[k_rows, :] += nn(prob_b, g_s[q_rows, :])
        dk_acc[k_rows, :] += nn(dscore_b, q_s[q_rows, :])
        dqt_acc[i] += nn(kt_s[c], dscore_b)

    def step(t, _):
        for u in range(0, UNROLL, 2):
            for opened in [open_tile(UNROLL * t + u), open_tile(UNROLL * t + u + 1)]:
                close_tile(*opened)
        return 0

    lax.fori_loop(0, (n_tiles + UNROLL - 1) // UNROLL, step, 0)
    for i in range(2 * n_q):
        dq = (dqt_acc[i] * scale).astype(BF).T
        for h in range(HQ):
            dq_refs[i // 2][(i % 2) * SPAN : (i % 2 + 1) * SPAN, h * HD : (h + 1) * HD] = dq[h * SPAN : (h + 1) * SPAN]
    for w in range(n_k):
        for s in range(2):
            at = pl.ds(pl.multiple_of(table[2 * w + s] * SPAN, SPAN), SPAN)
            dkv_ref[w, s * SPAN : (s + 1) * SPAN, :] = dk_acc[at, :].astype(BF)
            dkv_ref[w, TOK + s * SPAN : TOK + (s + 1) * SPAN, :] = dv_acc[at, :].astype(BF)


def tile_grads(table, q_blocks, gkv):
    n_q, n_k = len(q_blocks), gkv.shape[0]
    keys, rows = n_k * TOK, 2 * n_q * QROWS
    outs = pl.pallas_call(
        lambda *refs: tile_kernel(n_q, n_k, *refs),
        out_shape=[jax.ShapeDtypeStruct((TOK, HQ * HD), BF)] * n_q + [jax.ShapeDtypeStruct((n_k, 2 * TOK, HD), BF)],
        in_specs=[SMEM] + [VMEM] * (n_q + 1),
        out_specs=[VMEM] * (n_q + 1),
        scratch_shapes=[
            pltpu.VMEM((rows, HD), BF),
            pltpu.VMEM((rows, HD), BF),
            pltpu.VMEM((keys, HD), BF),
            pltpu.VMEM((keys, HD), BF),
            pltpu.VMEM((keys // CHUNK, HD, CHUNK), BF),
            pltpu.VMEM((keys, HD), F32),
            pltpu.VMEM((keys, HD), F32),
            pltpu.VMEM((2 * n_q, HD, QROWS), F32),
            pltpu.VMEM((2 * n_q, 8, QROWS), F32),
            pltpu.VMEM((2 * n_q, 8, QROWS), F32),
        ],
        compiler_params=pltpu.CompilerParams(vmem_limit_bytes=32 * 1024 * 1024),
        cost_estimate=pl.CostEstimate(flops=5_000_000_000, bytes_accessed=4_000_000, transcendentals=2_000_000),
        name="tile_grads",
    )(table, *q_blocks, gkv)
    return outs[:n_q], outs[n_q]


def partial_kernel(own_ref, other_ref, kept_ref, swapped_ref, out_ref):
    cols = out_ref.shape[2]
    for h in range(out_ref.shape[0]):
        rows = slice(h * cols, (h + 1) * cols)
        part = nt(own_ref[...], kept_ref[rows, :]) + nt(other_ref[...], swapped_ref[rows, :])
        out_ref[h] = part.astype(BF)


def partial_hidden(own, other, kept, swapped, n_hi):
    return pl.pallas_call(
        partial_kernel,
        out_shape=jax.ShapeDtypeStruct((n_hi, own.shape[0], kept.shape[0] // n_hi), BF),
        in_specs=[VMEM] * 4,
        out_specs=VMEM,
        compiler_params=pltpu.CompilerParams(vmem_limit_bytes=16 * 1024 * 1024),
        name="partial_hidden",
    )(own, other, kept, swapped)


def prep(span_order, queries, grad_out, fwd_out, log_norm):
    return pl.pallas_call(
        prep_kernel,
        out_shape=jax.ShapeDtypeStruct((QBLOCK, HD), BF),
        in_specs=[SMEM, VMEM, VMEM, VMEM, VMEM],
        out_specs=VMEM,
        name="prep",
    )(span_order, queries, grad_out, fwd_out, log_norm)


def pack(span_order, key_rows, value_rows, copies):
    return pl.pallas_call(
        pack_kernel,
        out_shape=jax.ShapeDtypeStruct((copies, KBLOCK, HD), BF),
        in_specs=[SMEM, VMEM, VMEM],
        out_specs=VMEM,
        name="pack",
    )(span_order, key_rows, value_rows)


def hop(block, axis, shift):
    n = lax.axis_size(axis)
    return lax.ppermute(block, axis, [(i, (i + shift) % n) for i in range(n)])


def make_table(q_span, k_span, doc_lengths):
    boundary = doc_lengths[0]
    spans_k, spans_q = k_span.shape[0], q_span.shape[0]
    rank = jnp.sum((k_span[None, :] < k_span[:, None]).astype(jnp.int32), axis=1)
    slots = jnp.arange(spans_k, dtype=jnp.int32)
    in_order = jnp.sum(jnp.where(rank[None, :] == slots[:, None], k_span[None, :], 0), axis=1)
    first = jnp.where(q_span * SPAN >= boundary, boundary // SPAN, 0)
    low = jnp.sum((k_span[None, :] < first[:, None]).astype(jnp.int32), axis=1) // PER
    high = (jnp.sum((k_span[None, :] <= q_span[:, None]).astype(jnp.int32), axis=1) + PER - 1) // PER
    count = high - low
    places = jnp.arange(spans_q, dtype=jnp.int32)
    end = jnp.sum(jnp.where(places[None, :] <= places[:, None], count[None, :], 0), axis=1)
    tiles = jnp.arange(spans_q * spans_k // PER, dtype=jnp.int32)
    place = jnp.sum((tiles[:, None] >= end[None, :]).astype(jnp.int32), axis=1)
    mine = place[:, None] == places[None, :]
    chunk = jnp.sum(jnp.where(mine, tiles[:, None] + (high - end)[None, :], 0), axis=1)
    span = jnp.sum(jnp.where(mine, q_span[None, :], 0), axis=1)
    unused = place == spans_q
    span = jnp.where(unused, -SPAN * spans_k * 1024, span)
    work = jnp.stack([span, jnp.where(unused, 0, place), chunk], axis=1).reshape(-1)
    return jnp.concatenate([rank, in_order, work, boundary[None], end[-1:]])


def body(queries, key_rows, value_rows, grad_out, fwd_out, log_norm, span_order, doc_lengths, key_proj, value_proj):
    n_q, n_k = lax.axis_size("x"), lax.axis_size(KEYS)
    n_hi = lax.axis_size("y_hi")
    scale = 1.0 / math.sqrt(HD)
    core = lax.axis_index("core")
    y_hi = lax.axis_index("y_hi")

    gkv = lax.all_to_all(pack(span_order, key_rows, value_rows, n_k), KEYS, 0, 0)
    mine = prep(span_order, queries, grad_out, fwd_out, log_norm)
    q_blocks = [mine] + [hop(mine, "x", shift) for shift in range(1, n_q)]

    cols = key_proj.shape[0] // (2 * n_hi)
    projs = jnp.concatenate([key_proj, value_proj], axis=1).reshape(n_hi, 2, cols, 2 * HD)
    kept = lax.dynamic_index_in_dim(projs, core, 1, keepdims=False).reshape(n_hi * cols, 2 * HD)
    given = lax.dynamic_index_in_dim(projs, 1 - core, 1, keepdims=False).reshape(n_hi * cols, 2 * HD)
    swapped = hop(given, "core", 1)

    tags = jnp.stack([b[2 * HQ * TOK + 24 : 2 * HQ * TOK + 26, 0] for b in q_blocks])
    q_span = tags.reshape(2 * n_q).astype(jnp.int32)
    k_span = gkv[:, 2 * TOK : 2 * TOK + 2, 0].reshape(2 * n_k).astype(jnp.int32)
    dqs, dkv = tile_grads(make_table(q_span, k_span, doc_lengths), q_blocks, gkv)

    parts = lax.all_to_all(dkv, KEYS, 0, 0)
    homes = [dqs[0]] + [hop(dqs[shift], "x", -shift) for shift in range(1, n_q)]
    parts, homes, swapped = lax.optimization_barrier((parts, homes, swapped))
    grad_query = sum(h.astype(F32) for h in homes).astype(BF)
    total = jnp.sum(parts.astype(F32), axis=0)
    grad_key = (total[:TOK] * scale).astype(BF)
    grad_value = total[TOK:].astype(BF)

    both = jnp.concatenate([grad_key, grad_value], axis=1)
    partial = partial_hidden(both, hop(both, "core", 1), kept, swapped, n_hi)
    shares = lax.all_to_all(partial, "y_hi", 0, 0)
    hidden = jnp.sum(shares.astype(F32), axis=0).astype(BF)
    return grad_query, grad_key, grad_value, hidden


def solution(mesh):
    fine = Mesh(mesh.devices.reshape(4, 2, 8, 4, 2), AXES)
    placed = (
        P(CTX, KV),
        P(CTX, KV),
        P(CTX, KV),
        P(CTX, KV),
        P(CTX, KV),
        P(KV, CTX),
        P(CTX),
        P(),
        P(None, KV),
        P(None, KV),
    )
    return jax.shard_map(
        body,
        mesh=fine,
        in_specs=placed,
        out_specs=(P(CTX, KV), P(CTX, KV), P(CTX, KV), P(CTX, KV)),
        check_vma=False,
    )
```

```python
import math

import jax
import jax.numpy as jnp
from jax import lax
from jax.experimental import pallas as pl
from jax.experimental.pallas import tpu as pltpu
from jax.sharding import Mesh, PartitionSpec as P

AXES = ("x", "y_lo", "z", "y_hi", "core")
CTX = ("x", "y_lo", "z")
KEYS = ("y_lo", "z")
KV = ("y_hi", "core")
SPAN = 64
HD = 128
HQ = 4
TOK = 2 * SPAN
QROWS = HQ * SPAN
CHUNK = 256
UNROLL = 4
PER = CHUNK // SPAN
QBLOCK = 2 * HQ * TOK + 32
KBLOCK = 2 * TOK + 16
BF = jnp.bfloat16
F32 = jnp.float32
VMEM = pl.BlockSpec(memory_space=pltpu.VMEM)
SMEM = pl.BlockSpec(memory_space=pltpu.SMEM)


def nt(a, b):
    return lax.dot_general(a, b, (((1,), (1,)), ((), ())), preferred_element_type=F32)


def nn(a, b):
    return lax.dot_general(a, b, (((1,), (0,)), ((), ())), preferred_element_type=F32)


def span_lines(span_ref, lines):
    line = lax.broadcasted_iota(jnp.int32, (lines, HD), 0)
    return jnp.where(line & 1 == 0, span_ref[0], span_ref[1]).astype(F32)


def pack_kernel(span_ref, k_ref, v_ref, out_ref, block, sem):
    block[:TOK, :] = k_ref[...]
    block[TOK : 2 * TOK, :] = v_ref[...]
    block[2 * TOK :, :] = span_lines(span_ref, KBLOCK - 2 * TOK).astype(BF)
    copies = [pltpu.make_async_copy(block, out_ref.at[w], sem.at[w]) for w in range(out_ref.shape[0])]
    for copy in copies:
        copy.start()
    for copy in copies:
        copy.wait()


def prep_kernel(span_ref, q_ref, g_ref, o_ref, lse_ref, out_ref, kept_ref):
    lse_rows, delta_rows = [], []
    for s in range(2):
        rows = slice(s * SPAN, (s + 1) * SPAN)
        for pair in range(HQ // 2):
            prods = []
            for h in (2 * pair, 2 * pair + 1):
                cols = slice(h * HD, (h + 1) * HD)
                at = s * QROWS + h * SPAN
                g = g_ref[rows, cols]
                out_ref[at : at + SPAN, :] = q_ref[rows, cols]
                out_ref[HQ * TOK + at : HQ * TOK + at + SPAN, :] = g
                prods.append(g.astype(F32) * o_ref[rows, cols].astype(F32))
            both = jnp.concatenate(prods, axis=0)
            delta_rows.append(jnp.sum(both.T, axis=0, keepdims=True))
            lse_rows.append(
                jnp.concatenate(
                    [lse_ref[2 * pair : 2 * pair + 1, rows], lse_ref[2 * pair + 1 : 2 * pair + 2, rows]],
                    axis=1,
                )
            )
    parts = []
    for rows in (lse_rows, delta_rows):
        rest = jnp.concatenate(rows, axis=0)
        for _ in range(3):
            piece = rest.astype(BF).astype(F32)
            rest = rest - piece
            parts.append(piece)
    parts.append(span_lines(span_ref, 8))
    out_ref[2 * HQ * TOK :, :] = jnp.concatenate(parts, axis=0).astype(BF)
    kept_ref[...] = jnp.concatenate(parts[:6], axis=0)


def plan_tiles(span_ref, other_blocks, gkv_ref, boundary):
    spans_q, spans_k = 2 * len(other_blocks) + 2, 2 * gkv_ref.shape[0]
    lines = max(spans_q, spans_k, 16)
    sub = lax.broadcasted_iota(jnp.int32, (lines, HD), 0)
    lane = lax.broadcasted_iota(jnp.int32, (lines, HD), 1)

    def column(tags):
        out = jnp.full((lines, HD), -1.0, F32)
        for b, tag in enumerate(tags):
            tag = tag.astype(F32)
            out = jnp.where(sub >> 1 == b, jnp.concatenate([tag] * (lines // tag.shape[0]), axis=0), out)
        return out.astype(jnp.int32)

    def total(rows):
        return jnp.sum(rows, axis=0, keepdims=True)

    k = column([gkv_ref[w, 2 * TOK : 2 * TOK + 16, :] for w in range(spans_k // 2)])
    q = column([span_lines(span_ref, 8)] + [block[2 * HQ * TOK + 16 : 2 * HQ * TOK + 32, :][8:] for block in other_blocks])
    first = jnp.where(q * SPAN >= boundary, boundary >> 6, 0)
    zero = jnp.zeros((lines, HD), jnp.int32)
    rank, below, upto = zero, zero, zero
    for j in range(spans_k):
        one = k[j : j + 1]
        rank = rank + (one < k).astype(jnp.int32)
        below = below + (one < first).astype(jnp.int32)
        upto = upto + (one <= q).astype(jnp.int32)
    real_k = sub < spans_k
    rank_line = total(jnp.where((lane == sub) & real_k, rank, 0))
    in_order = total(jnp.where((lane == rank) & real_k, k, 0))
    shift = PER.bit_length() - 1
    low, high = below >> shift, (upto + PER - 1) >> shift
    count = jnp.where(sub < spans_q, high - low, 0)
    end = zero
    for i in range(spans_q):
        end = end + jnp.where(sub >= i, count[i : i + 1], 0)
    place = total(jnp.where((lane >= end) & (sub < spans_q), 1, 0))
    mine = sub == place
    chunk = lane[:1] + total(jnp.where(mine, high - end, 0))
    span = total(jnp.where(mine, q, 0))
    unused = place >= spans_q
    span = jnp.where(unused, -(1 << 20), span)
    chunk = jnp.where(unused, 0, chunk)
    place = jnp.where(unused, 0, place)
    n_tiles = end[spans_q - 1 : spans_q]
    return jnp.concatenate([rank_line, in_order, span, place, chunk, n_tiles, n_tiles, n_tiles], axis=0)


def tile_kernel(n_q, n_x, n_k, doc_ref, span_ref, *refs):
    (own_q, own_g, own_rows), other_blocks, gkv_ref, refs = refs[:3], refs[3 : n_q + 2], refs[n_q + 2], refs[n_q + 3 :]
    dq_refs, dkv_out, refs = refs[:n_x], refs[n_x], refs[n_x + 1 :]
    dkv_ref, plan_v, plan_s, sems, q_s, g_s, k_s, v_s, kt_s, dk_acc, dv_acc, dqt_acc, lse_s, del_s = refs
    spans_k = 2 * n_k
    scale = 1.0 / math.sqrt(HD)
    log2e = 1.0 / math.log(2.0)
    boundary = doc_ref[0]

    plan_v[...] = plan_tiles(span_ref, other_blocks, gkv_ref, boundary)
    tell = pltpu.make_async_copy(plan_v, plan_s, sems.at[0])
    tell.start()
    dk_acc[...] = jnp.zeros_like(dk_acc)
    dv_acc[...] = jnp.zeros_like(dv_acc)
    dqt_acc[...] = jnp.zeros_like(dqt_acc)
    for s in range(2):
        for h in range(HQ):
            at = s * QROWS + h * SPAN
            rows, cols = slice(s * SPAN, (s + 1) * SPAN), slice(h * HD, (h + 1) * HD)
            q_s[at : at + SPAN, :] = own_q[rows, cols]
            g_s[at : at + SPAN, :] = own_g[rows, cols]
    for b in range(n_q):
        if b == 0:
            extra = own_rows[...]
        else:
            block = other_blocks[b - 1]
            q_s[b * 2 * QROWS : (b + 1) * 2 * QROWS, :] = block[: HQ * TOK, :]
            g_s[b * 2 * QROWS : (b + 1) * 2 * QROWS, :] = block[HQ * TOK : 2 * HQ * TOK, :]
            extra = block[2 * HQ * TOK : 2 * HQ * TOK + 24, :].astype(F32)
        lse = (extra[0:4] + extra[4:8] + extra[8:12]) * log2e
        dlt = extra[12:16] + extra[16:20] + extra[20:24]
        for s in range(2):
            i = 2 * b + s
            lse_s[i] = jnp.broadcast_to(jnp.concatenate([lse[2 * s : 2 * s + 1], lse[2 * s + 1 : 2 * s + 2]], axis=1), (8, QROWS))
            del_s[i] = jnp.broadcast_to(jnp.concatenate([dlt[2 * s : 2 * s + 1], dlt[2 * s + 1 : 2 * s + 2]], axis=1), (8, QROWS))
    tell.wait()
    n_tiles = plan_s[5, 0]
    for w in range(n_k):
        for s in range(2):
            to = pl.ds(pl.multiple_of(plan_s[0, 2 * w + s] * SPAN, SPAN), SPAN)
            k_s[to, :] = gkv_ref[w, s * SPAN : (s + 1) * SPAN, :]
            v_s[to, :] = gkv_ref[w, TOK + s * SPAN : TOK + (s + 1) * SPAN, :]
    for c in range(spans_k // PER):
        kt_s[c] = k_s[c * CHUNK : (c + 1) * CHUNK, :].T

    key_line = lax.broadcasted_iota(jnp.int32, (SPAN, QROWS), 0)
    row_off = lax.broadcasted_iota(jnp.int32, (1, QROWS), 1) % SPAN

    def open_tile(t):
        span, i, c = plan_s[2, t], plan_s[3, t], plan_s[4, t]
        q_rows = pl.ds(pl.multiple_of(i * QROWS, QROWS), QROWS)
        k_rows = pl.ds(pl.multiple_of(c * CHUNK, CHUNK), CHUNK)
        score = nt(k_s[k_rows, :], q_s[q_rows, :])
        dprob = nt(v_s[k_rows, :], g_s[q_rows, :])
        lse, dlt = lse_s[i][0:1], del_s[i][0:1]
        q_pos = span * SPAN + row_off
        q_start = jnp.where(q_pos >= boundary, boundary, 0)
        probs, dscores = [], []
        for j in range(PER):
            part = slice(j * SPAN, (j + 1) * SPAN)
            base = plan_s[1, c * PER + j] * SPAN
            live = (key_line <= q_pos - base) & (key_line >= q_start - base)
            prob = jnp.where(live, jnp.exp2(score[part] * (scale * log2e) - lse), 0.0)
            probs.append(prob.astype(BF))
            dscores.append((prob * (dprob[part] - dlt)).astype(BF))
        return i, c, q_rows, k_rows, jnp.concatenate(probs, axis=0), jnp.concatenate(dscores, axis=0)

    def close_tile(i, c, q_rows, k_rows, prob_b, dscore_b):
        dv_acc[k_rows, :] += nn(prob_b, g_s[q_rows, :])
        dk_acc[k_rows, :] += nn(dscore_b, q_s[q_rows, :])
        dqt_acc[i] += nn(kt_s[c], dscore_b)

    def step(t, _):
        for u in range(0, UNROLL, 2):
            for opened in [open_tile(UNROLL * t + u), open_tile(UNROLL * t + u + 1)]:
                close_tile(*opened)
        return 0

    lax.fori_loop(0, (n_tiles + UNROLL - 1) // UNROLL, step, 0)
    sends = []
    for w in range(n_k):
        for s in range(2):
            at = pl.ds(pl.multiple_of(plan_s[0, 2 * w + s] * SPAN, SPAN), SPAN)
            dkv_ref[w, s * SPAN : (s + 1) * SPAN, :] = dk_acc[at, :].astype(BF)
            dkv_ref[w, TOK + s * SPAN : TOK + (s + 1) * SPAN, :] = dv_acc[at, :].astype(BF)
        if w % 4 == 3:
            some = pl.ds(w - 3, 4)
            sends.append(pltpu.make_async_copy(dkv_ref.at[some], dkv_out.at[some], sems.at[1 + w // 4]))
            sends[-1].start()
    for i in range(2 * n_q):
        dq = (dqt_acc[i] * scale).astype(BF).T
        place, s = i // 2, i % 2
        at = place // n_x * TOK + s * SPAN
        for h in range(HQ):
            dq_refs[place % n_x][at : at + SPAN, h * HD : (h + 1) * HD] = dq[h * SPAN : (h + 1) * SPAN]
    for send in sends:
        send.wait()


def tile_grads(doc_lengths, span_order, own, q_blocks, gkv, n_x):
    n_q, n_k = len(q_blocks) + 1, gkv.shape[0]
    keys, rows = n_k * TOK, 2 * n_q * QROWS
    outs = pl.pallas_call(
        lambda *refs: tile_kernel(n_q, n_x, n_k, *refs),
        out_shape=[jax.ShapeDtypeStruct((n_q // n_x * TOK, HQ * HD), BF)] * n_x + [jax.ShapeDtypeStruct((n_k, 2 * TOK, HD), BF)],
        in_specs=[SMEM, SMEM] + [VMEM] * (n_q + 3),
        out_specs=[VMEM] * n_x + [pl.BlockSpec(memory_space=pl.ANY)],
        scratch_shapes=[
            pltpu.VMEM((n_k, 2 * TOK, HD), BF),
            pltpu.VMEM((8, HD), jnp.int32),
            pltpu.SMEM((8, HD), jnp.int32),
            pltpu.SemaphoreType.DMA((1 + n_k // 4,)),
            pltpu.VMEM((rows, HD), BF),
            pltpu.VMEM((rows, HD), BF),
            pltpu.VMEM((keys, HD), BF),
            pltpu.VMEM((keys, HD), BF),
            pltpu.VMEM((keys // CHUNK, HD, CHUNK), BF),
            pltpu.VMEM((keys, HD), F32),
            pltpu.VMEM((keys, HD), F32),
            pltpu.VMEM((2 * n_q, HD, QROWS), F32),
            pltpu.VMEM((2 * n_q, 8, QROWS), F32),
            pltpu.VMEM((2 * n_q, 8, QROWS), F32),
        ],
        compiler_params=pltpu.CompilerParams(vmem_limit_bytes=32 * 1024 * 1024),
        cost_estimate=pl.CostEstimate(flops=5_000_000_000, bytes_accessed=4_000_000, transcendentals=2_000_000),
        name="tile_grads",
    )(doc_lengths, span_order, *own, *q_blocks, gkv)
    return outs[:n_x], outs[n_x]


def partial_kernel(own_ref, other_ref, swapped_ref, out_ref):
    cols = out_ref.shape[2]
    for h in range(out_ref.shape[0]):
        at = slice(h * cols, (h + 1) * cols)
        out_ref[h] = (own_ref[:, at] + nt(other_ref[...], swapped_ref[at, :])).astype(BF)


def partial_hidden(own, other, swapped, n_hi):
    return pl.pallas_call(
        partial_kernel,
        out_shape=jax.ShapeDtypeStruct((n_hi, own.shape[0], own.shape[1] // n_hi), BF),
        in_specs=[VMEM] * 3,
        out_specs=VMEM,
        compiler_params=pltpu.CompilerParams(vmem_limit_bytes=16 * 1024 * 1024),
        name="partial_hidden",
    )(own, other, swapped)


def prep(span_order, queries, grad_out, fwd_out, log_norm):
    return pl.pallas_call(
        prep_kernel,
        out_shape=[jax.ShapeDtypeStruct((QBLOCK, HD), BF), jax.ShapeDtypeStruct((24, HD), F32)],
        in_specs=[SMEM, VMEM, VMEM, VMEM, VMEM],
        out_specs=[VMEM] * 2,
        name="prep",
    )(span_order, queries, grad_out, fwd_out, log_norm)


def pack(span_order, key_rows, value_rows, copies):
    return pl.pallas_call(
        pack_kernel,
        out_shape=jax.ShapeDtypeStruct((copies, KBLOCK, HD), BF),
        in_specs=[SMEM, VMEM, VMEM],
        out_specs=pl.BlockSpec(memory_space=pl.ANY),
        scratch_shapes=[pltpu.VMEM((KBLOCK, HD), BF), pltpu.SemaphoreType.DMA((copies,))],
        name="pack",
    )(span_order, key_rows, value_rows)


def hop(block, axis, shift):
    n = lax.axis_size(axis)
    return lax.ppermute(block, axis, [(i, (i + shift) % n) for i in range(n)])


def body(queries, key_rows, value_rows, grad_out, fwd_out, log_norm, span_order, doc_lengths, key_proj, value_proj):
    n_q, n_k = lax.axis_size("x"), lax.axis_size(KEYS)
    n_hi = lax.axis_size("y_hi")
    core = lax.axis_index("core")

    gkv = lax.all_to_all(pack(span_order, key_rows, value_rows, n_k), KEYS, 0, 0)
    mine, own_rows = prep(span_order, queries, grad_out, fwd_out, log_norm)
    q_blocks = [hop(mine, "x", shift) for shift in range(1, n_q)]

    cols = key_proj.shape[0] // (2 * n_hi)
    projs = jnp.concatenate([key_proj, value_proj], axis=1).reshape(n_hi, 2, cols, 2 * HD)
    kept = lax.dynamic_index_in_dim(projs, core, 1, keepdims=False).reshape(n_hi * cols, 2 * HD)
    given = lax.dynamic_index_in_dim(projs, 1 - core, 1, keepdims=False).reshape(n_hi * cols, 2 * HD)
    swapped = hop(given, "core", 1)

    dqs, dkv = tile_grads(doc_lengths, span_order, (queries, grad_out, own_rows), q_blocks, gkv, n_q)

    parts = lax.all_to_all(dkv, KEYS, 0, 0)
    homes = [dqs[0]] + [hop(dqs[shift], "x", -shift) for shift in range(1, n_q)]
    parts, homes, swapped = lax.optimization_barrier((parts, homes, swapped))
    grad_query = sum(h.astype(F32) for h in homes).astype(BF)
    total = jnp.sum(parts.astype(F32), axis=0)
    grad_key = (total[:TOK] * (1.0 / math.sqrt(HD))).astype(BF)
    grad_value = total[TOK:].astype(BF)
    both = jnp.concatenate([grad_key, grad_value], axis=1)

    partial = partial_hidden(nt(both, kept), hop(both, "core", 1), swapped, n_hi)
    shares = lax.all_to_all(partial, "y_hi", 0, 0)
    hidden = jnp.sum(shares.astype(F32), axis=0).astype(BF)
    return grad_query, grad_key, grad_value, hidden


def solution(mesh):
    fine = Mesh(mesh.devices.reshape(4, 2, 8, 4, 2), AXES)
    placed = (
        P(CTX, KV),
        P(CTX, KV),
        P(CTX, KV),
        P(CTX, KV),
        P(CTX, KV),
        P(KV, CTX),
        P(CTX),
        P(),
        P(None, KV),
        P(None, KV),
    )
    return jax.shard_map(
        body,
        mesh=fine,
        in_specs=placed,
        out_specs=(P(CTX, KV), P(CTX, KV), P(CTX, KV), P(CTX, KV)),
        check_vma=False,
    )
```

```python
import math

import jax
import jax.numpy as jnp
from jax import lax
from jax.experimental import pallas as pl
from jax.experimental.pallas import tpu as pltpu
from jax.sharding import Mesh, PartitionSpec as P

AXES = ("x", "y_lo", "z", "y_hi", "core")
CTX = ("x", "y_lo", "z")
KEYS = ("z", "y_lo")
KV = ("y_hi", "core")
SPAN = 64
HD = 128
HQ = 4
TOK = 2 * SPAN
QROWS = HQ * SPAN
CHUNK = 256
UNROLL = 4
PER = CHUNK // SPAN
QBLOCK = 2 * HQ * TOK + 32
KBLOCK = 2 * TOK + 16
BF = jnp.bfloat16
F32 = jnp.float32
VMEM = pl.BlockSpec(memory_space=pltpu.VMEM)
SMEM = pl.BlockSpec(memory_space=pltpu.SMEM)


def nt(a, b):
    return lax.dot_general(a, b, (((1,), (1,)), ((), ())), preferred_element_type=F32)


def nn(a, b):
    return lax.dot_general(a, b, (((1,), (0,)), ((), ())), preferred_element_type=F32)


def span_lines(span_ref, lines):
    line = lax.broadcasted_iota(jnp.int32, (lines, HD), 0)
    return jnp.where(line & 1 == 0, span_ref[0], span_ref[1]).astype(F32)


def pack_kernel(span_ref, k_ref, v_ref, out_ref, block, sem):
    block[:TOK, :] = k_ref[...]
    block[TOK : 2 * TOK, :] = v_ref[...]
    block[2 * TOK :, :] = span_lines(span_ref, KBLOCK - 2 * TOK).astype(BF)
    copies = [pltpu.make_async_copy(block, out_ref.at[w], sem.at[w]) for w in range(out_ref.shape[0])]
    for copy in copies:
        copy.start()
    for copy in copies:
        copy.wait()


def prep_kernel(span_ref, q_ref, g_ref, o_ref, lse_ref, out_ref, kept_ref):
    lse_rows, delta_rows = [], []
    for s in range(2):
        rows = slice(s * SPAN, (s + 1) * SPAN)
        for pair in range(HQ // 2):
            prods = []
            for h in (2 * pair, 2 * pair + 1):
                cols = slice(h * HD, (h + 1) * HD)
                at = s * QROWS + h * SPAN
                g = g_ref[rows, cols]
                out_ref[at : at + SPAN, :] = q_ref[rows, cols]
                out_ref[HQ * TOK + at : HQ * TOK + at + SPAN, :] = g
                prods.append(g.astype(F32) * o_ref[rows, cols].astype(F32))
            both = jnp.concatenate(prods, axis=0)
            delta_rows.append(jnp.sum(both.T, axis=0, keepdims=True))
            lse_rows.append(
                jnp.concatenate(
                    [lse_ref[2 * pair : 2 * pair + 1, rows], lse_ref[2 * pair + 1 : 2 * pair + 2, rows]],
                    axis=1,
                )
            )
    parts = []
    for rows in (lse_rows, delta_rows):
        rest = jnp.concatenate(rows, axis=0)
        for _ in range(3):
            piece = rest.astype(BF).astype(F32)
            rest = rest - piece
            parts.append(piece)
    parts.append(span_lines(span_ref, 8))
    out_ref[2 * HQ * TOK :, :] = jnp.concatenate(parts, axis=0).astype(BF)
    kept_ref[...] = jnp.concatenate(parts[:6], axis=0)


def plan_tiles(span_ref, other_blocks, gkv_ref, boundary):
    spans_q, spans_k = 2 * len(other_blocks) + 2, 2 * gkv_ref.shape[0]
    lines = max(spans_q, spans_k, 16)
    sub = lax.broadcasted_iota(jnp.int32, (lines, HD), 0)
    lane = lax.broadcasted_iota(jnp.int32, (lines, HD), 1)

    def column(tags):
        out = jnp.full((lines, HD), -1.0, F32)
        for b, tag in enumerate(tags):
            tag = tag.astype(F32)
            out = jnp.where(sub >> 1 == b, jnp.concatenate([tag] * (lines // tag.shape[0]), axis=0), out)
        return out.astype(jnp.int32)

    def total(rows):
        return jnp.sum(rows, axis=0, keepdims=True)

    k = column([gkv_ref[w, 2 * TOK : 2 * TOK + 16, :] for w in range(spans_k // 2)])
    q = column([span_lines(span_ref, 8)] + [block[2 * HQ * TOK + 16 : 2 * HQ * TOK + 32, :][8:] for block in other_blocks])
    first = jnp.where(q * SPAN >= boundary, boundary >> 6, 0)
    zero = jnp.zeros((lines, HD), jnp.int32)
    rank, below, upto = zero, zero, zero
    for j in range(spans_k):
        one = k[j : j + 1]
        rank = rank + (one < k).astype(jnp.int32)
        below = below + (one < first).astype(jnp.int32)
        upto = upto + (one <= q).astype(jnp.int32)
    real_k = sub < spans_k
    rank_line = total(jnp.where((lane == sub) & real_k, rank, 0))
    in_order = total(jnp.where((lane == rank) & real_k, k, 0))
    shift = PER.bit_length() - 1
    low, high = below >> shift, (upto + PER - 1) >> shift
    count = jnp.where(sub < spans_q, high - low, 0)
    end = zero
    for i in range(spans_q):
        end = end + jnp.where(sub >= i, count[i : i + 1], 0)
    place = total(jnp.where((lane >= end) & (sub < spans_q), 1, 0))
    mine = sub == place
    chunk = lane[:1] + total(jnp.where(mine, high - end, 0))
    span = total(jnp.where(mine, q, 0))
    unused = place >= spans_q
    span = jnp.where(unused, -(1 << 20), span)
    chunk = jnp.where(unused, 0, chunk)
    place = jnp.where(unused, 0, place)
    n_tiles = end[spans_q - 1 : spans_q]
    return jnp.concatenate([rank_line, in_order, span, place, chunk, n_tiles, n_tiles, n_tiles], axis=0)


def tile_kernel(n_q, n_x, n_k, doc_ref, span_ref, *refs):
    (own_q, own_g, own_rows), other_blocks, gkv_ref, refs = refs[:3], refs[3 : n_q + 2], refs[n_q + 2], refs[n_q + 3 :]
    dq_refs, dkv_out, refs = refs[:n_x], refs[n_x], refs[n_x + 1 :]
    dkv_ref, plan_v, plan_s, sems, q_s, g_s, k_s, v_s, kt_s, dk_acc, dv_acc, dqt_acc, lse_s, del_s = refs
    spans_k = 2 * n_k
    scale = 1.0 / math.sqrt(HD)
    log2e = 1.0 / math.log(2.0)
    boundary = doc_ref[0]

    plan_v[...] = plan_tiles(span_ref, other_blocks, gkv_ref, boundary)
    tell = pltpu.make_async_copy(plan_v, plan_s, sems.at[0])
    tell.start()
    dk_acc[...] = jnp.zeros_like(dk_acc)
    dv_acc[...] = jnp.zeros_like(dv_acc)
    dqt_acc[...] = jnp.zeros_like(dqt_acc)
    for s in range(2):
        for h in range(HQ):
            at = s * QROWS + h * SPAN
            rows, cols = slice(s * SPAN, (s + 1) * SPAN), slice(h * HD, (h + 1) * HD)
            q_s[at : at + SPAN, :] = own_q[rows, cols]
            g_s[at : at + SPAN, :] = own_g[rows, cols]
    for b in range(n_q):
        if b == 0:
            extra = own_rows[...]
        else:
            block = other_blocks[b - 1]
            q_s[b * 2 * QROWS : (b + 1) * 2 * QROWS, :] = block[: HQ * TOK, :]
            g_s[b * 2 * QROWS : (b + 1) * 2 * QROWS, :] = block[HQ * TOK : 2 * HQ * TOK, :]
            extra = block[2 * HQ * TOK : 2 * HQ * TOK + 24, :].astype(F32)
        lse = (extra[0:4] + extra[4:8] + extra[8:12]) * log2e
        dlt = extra[12:16] + extra[16:20] + extra[20:24]
        for s in range(2):
            i = 2 * b + s
            lse_s[i] = jnp.broadcast_to(jnp.concatenate([lse[2 * s : 2 * s + 1], lse[2 * s + 1 : 2 * s + 2]], axis=1), (8, QROWS))
            del_s[i] = jnp.broadcast_to(jnp.concatenate([dlt[2 * s : 2 * s + 1], dlt[2 * s + 1 : 2 * s + 2]], axis=1), (8, QROWS))
    tell.wait()
    n_tiles = plan_s[5, 0]
    for w in range(n_k):
        for s in range(2):
            to = pl.ds(pl.multiple_of(plan_s[0, 2 * w + s] * SPAN, SPAN), SPAN)
            k_s[to, :] = gkv_ref[w, s * SPAN : (s + 1) * SPAN, :]
            v_s[to, :] = gkv_ref[w, TOK + s * SPAN : TOK + (s + 1) * SPAN, :]
    for c in range(spans_k // PER):
        kt_s[c] = k_s[c * CHUNK : (c + 1) * CHUNK, :].T

    key_line = lax.broadcasted_iota(jnp.int32, (SPAN, QROWS), 0)
    row_off = lax.broadcasted_iota(jnp.int32, (1, QROWS), 1) % SPAN

    def open_tile(t):
        span, i, c = plan_s[2, t], plan_s[3, t], plan_s[4, t]
        q_rows = pl.ds(pl.multiple_of(i * QROWS, QROWS), QROWS)
        k_rows = pl.ds(pl.multiple_of(c * CHUNK, CHUNK), CHUNK)
        score = nt(k_s[k_rows, :], q_s[q_rows, :])
        dprob = nt(v_s[k_rows, :], g_s[q_rows, :])
        lse, dlt = lse_s[i][0:1], del_s[i][0:1]
        q_pos = span * SPAN + row_off
        q_start = jnp.where(q_pos >= boundary, boundary, 0)
        probs, dscores = [], []
        for j in range(PER):
            part = slice(j * SPAN, (j + 1) * SPAN)
            base = plan_s[1, c * PER + j] * SPAN
            live = (key_line <= q_pos - base) & (key_line >= q_start - base)
            prob = jnp.where(live, jnp.exp2(score[part] * (scale * log2e) - lse), 0.0)
            probs.append(prob.astype(BF))
            dscores.append((prob * (dprob[part] - dlt)).astype(BF))
        return i, c, q_rows, k_rows, jnp.concatenate(probs, axis=0), jnp.concatenate(dscores, axis=0)

    def close_tile(i, c, q_rows, k_rows, prob_b, dscore_b):
        dv_acc[k_rows, :] += nn(prob_b, g_s[q_rows, :])
        dk_acc[k_rows, :] += nn(dscore_b, q_s[q_rows, :])
        dqt_acc[i] += nn(kt_s[c], dscore_b)

    def step(t, _):
        for u in range(0, UNROLL, 2):
            for opened in [open_tile(UNROLL * t + u), open_tile(UNROLL * t + u + 1)]:
                close_tile(*opened)
        return 0

    lax.fori_loop(0, (n_tiles + UNROLL - 1) // UNROLL, step, 0)
    sends = []
    for w in range(n_k):
        for s in range(2):
            at = pl.ds(pl.multiple_of(plan_s[0, 2 * w + s] * SPAN, SPAN), SPAN)
            dkv_ref[w, s * SPAN : (s + 1) * SPAN, :] = dk_acc[at, :].astype(BF)
            dkv_ref[w, TOK + s * SPAN : TOK + (s + 1) * SPAN, :] = dv_acc[at, :].astype(BF)
        if w % 4 == 3:
            some = pl.ds(w - 3, 4)
            sends.append(pltpu.make_async_copy(dkv_ref.at[some], dkv_out.at[some], sems.at[1 + w // 4]))
            sends[-1].start()
    for i in range(2 * n_q):
        dq = (dqt_acc[i] * scale).astype(BF).T
        place, s = i // 2, i % 2
        at = place // n_x * TOK + s * SPAN
        for h in range(HQ):
            dq_refs[place % n_x][at : at + SPAN, h * HD : (h + 1) * HD] = dq[h * SPAN : (h + 1) * SPAN]
    for send in sends:
        send.wait()


def tile_grads(doc_lengths, span_order, own, q_blocks, gkv, n_x):
    n_q, n_k = len(q_blocks) + 1, gkv.shape[0]
    keys, rows = n_k * TOK, 2 * n_q * QROWS
    outs = pl.pallas_call(
        lambda *refs: tile_kernel(n_q, n_x, n_k, *refs),
        out_shape=[jax.ShapeDtypeStruct((n_q // n_x * TOK, HQ * HD), BF)] * n_x + [jax.ShapeDtypeStruct((n_k, 2 * TOK, HD), BF)],
        in_specs=[SMEM, SMEM] + [VMEM] * (n_q + 3),
        out_specs=[VMEM] * n_x + [pl.BlockSpec(memory_space=pl.ANY)],
        scratch_shapes=[
            pltpu.VMEM((n_k, 2 * TOK, HD), BF),
            pltpu.VMEM((8, HD), jnp.int32),
            pltpu.SMEM((8, HD), jnp.int32),
            pltpu.SemaphoreType.DMA((1 + n_k // 4,)),
            pltpu.VMEM((rows, HD), BF),
            pltpu.VMEM((rows, HD), BF),
            pltpu.VMEM((keys, HD), BF),
            pltpu.VMEM((keys, HD), BF),
            pltpu.VMEM((keys // CHUNK, HD, CHUNK), BF),
            pltpu.VMEM((keys, HD), F32),
            pltpu.VMEM((keys, HD), F32),
            pltpu.VMEM((2 * n_q, HD, QROWS), F32),
            pltpu.VMEM((2 * n_q, 8, QROWS), F32),
            pltpu.VMEM((2 * n_q, 8, QROWS), F32),
        ],
        compiler_params=pltpu.CompilerParams(vmem_limit_bytes=32 * 1024 * 1024),
        cost_estimate=pl.CostEstimate(flops=5_000_000_000, bytes_accessed=4_000_000, transcendentals=2_000_000),
        name="tile_grads",
    )(doc_lengths, span_order, *own, *q_blocks, gkv)
    return outs[:n_x], outs[n_x]


def partial_kernel(own_ref, other_ref, swapped_ref, out_ref):
    cols = out_ref.shape[2]
    for h in range(out_ref.shape[0]):
        at = slice(h * cols, (h + 1) * cols)
        out_ref[h] = (own_ref[:, at] + nt(other_ref[...], swapped_ref[at, :])).astype(BF)


def partial_hidden(own, other, swapped, n_hi):
    return pl.pallas_call(
        partial_kernel,
        out_shape=jax.ShapeDtypeStruct((n_hi, own.shape[0], own.shape[1] // n_hi), BF),
        in_specs=[VMEM] * 3,
        out_specs=VMEM,
        compiler_params=pltpu.CompilerParams(vmem_limit_bytes=16 * 1024 * 1024),
        name="partial_hidden",
    )(own, other, swapped)


def prep(span_order, queries, grad_out, fwd_out, log_norm):
    return pl.pallas_call(
        prep_kernel,
        out_shape=[jax.ShapeDtypeStruct((QBLOCK, HD), BF), jax.ShapeDtypeStruct((24, HD), F32)],
        in_specs=[SMEM, VMEM, VMEM, VMEM, VMEM],
        out_specs=[VMEM] * 2,
        name="prep",
    )(span_order, queries, grad_out, fwd_out, log_norm)


def pack(span_order, key_rows, value_rows, copies):
    return pl.pallas_call(
        pack_kernel,
        out_shape=jax.ShapeDtypeStruct((copies, KBLOCK, HD), BF),
        in_specs=[SMEM, VMEM, VMEM],
        out_specs=pl.BlockSpec(memory_space=pl.ANY),
        scratch_shapes=[pltpu.VMEM((KBLOCK, HD), BF), pltpu.SemaphoreType.DMA((copies,))],
        name="pack",
    )(span_order, key_rows, value_rows)


def hop(block, axis, shift):
    n = lax.axis_size(axis)
    return lax.ppermute(block, axis, [(i, (i + shift) % n) for i in range(n)])


def body(queries, key_rows, value_rows, grad_out, fwd_out, log_norm, span_order, doc_lengths, key_proj, value_proj):
    n_q, n_k = lax.axis_size("x"), lax.axis_size(KEYS)
    n_hi = lax.axis_size("y_hi")
    core = lax.axis_index("core")

    gkv = lax.all_to_all(pack(span_order, key_rows, value_rows, n_k), KEYS, 0, 0)
    mine, own_rows = prep(span_order, queries, grad_out, fwd_out, log_norm)
    q_blocks = [hop(mine, "x", shift) for shift in range(1, n_q)]

    cols = key_proj.shape[0] // (2 * n_hi)
    projs = jnp.concatenate([key_proj, value_proj], axis=1).reshape(n_hi, 2, cols, 2 * HD)
    kept = lax.dynamic_index_in_dim(projs, core, 1, keepdims=False).reshape(n_hi * cols, 2 * HD)
    given = lax.dynamic_index_in_dim(projs, 1 - core, 1, keepdims=False).reshape(n_hi * cols, 2 * HD)
    swapped = hop(given, "core", 1)

    dqs, dkv = tile_grads(doc_lengths, span_order, (queries, grad_out, own_rows), q_blocks, gkv, n_q)

    parts = lax.all_to_all(dkv, KEYS, 0, 0)
    homes = [dqs[0]] + [hop(dqs[shift], "x", -shift) for shift in range(1, n_q)]
    parts, homes, swapped = lax.optimization_barrier((parts, homes, swapped))
    grad_query = sum(h.astype(F32) for h in homes).astype(BF)
    total = jnp.sum(parts.astype(F32), axis=0)
    grad_key = (total[:TOK] * (1.0 / math.sqrt(HD))).astype(BF)
    grad_value = total[TOK:].astype(BF)
    both = jnp.concatenate([grad_key, grad_value], axis=1)

    partial = partial_hidden(nt(both, kept), hop(both, "core", 1), swapped, n_hi)
    shares = lax.all_to_all(partial, "y_hi", 0, 0)
    hidden = jnp.sum(shares.astype(F32), axis=0).astype(BF)
    return grad_query, grad_key, grad_value, hidden


def solution(mesh):
    fine = Mesh(mesh.devices.reshape(4, 2, 8, 4, 2), AXES)
    placed = (
        P(CTX, KV),
        P(CTX, KV),
        P(CTX, KV),
        P(CTX, KV),
        P(CTX, KV),
        P(KV, CTX),
        P(CTX),
        P(),
        P(None, KV),
        P(None, KV),
    )
    return jax.shard_map(
        body,
        mesh=fine,
        in_specs=placed,
        out_specs=(P(CTX, KV), P(CTX, KV), P(CTX, KV), P(CTX, KV)),
        check_vma=False,
    )
```

```python
import math

import jax
import jax.numpy as jnp
from jax import lax
from jax.experimental import pallas as pl
from jax.experimental.pallas import tpu as pltpu
from jax.sharding import Mesh, PartitionSpec as P

AXES = ("x", "y_lo", "z", "y_hi", "core")
CTX = ("x", "y_lo", "z")
KEYS = ("z", "y_lo")
KV = ("y_hi", "core")
SPAN = 64
HD = 128
HQ = 4
TOK = 2 * SPAN
QROWS = HQ * SPAN
CHUNK = 256
UNROLL = 4
PER = CHUNK // SPAN
QBLOCK = 2 * HQ * TOK + 32
KBLOCK = 2 * TOK + 16
BF = jnp.bfloat16
F32 = jnp.float32
VMEM = pl.BlockSpec(memory_space=pltpu.VMEM)
SMEM = pl.BlockSpec(memory_space=pltpu.SMEM)


def nt(a, b):
    return lax.dot_general(a, b, (((1,), (1,)), ((), ())), preferred_element_type=F32)


def tn(a, b):
    return lax.dot_general(a, b, (((0,), (0,)), ((), ())), preferred_element_type=F32)


def nn(a, b):
    return lax.dot_general(a, b, (((1,), (0,)), ((), ())), preferred_element_type=F32)


def span_lines(span_ref, lines):
    line = lax.broadcasted_iota(jnp.int32, (lines, HD), 0)
    return jnp.where(line & 1 == 0, span_ref[0], span_ref[1]).astype(F32)


def pack_kernel(span_ref, k_ref, v_ref, out_ref, block, sem):
    block[:TOK, :] = k_ref[...]
    block[TOK : 2 * TOK, :] = v_ref[...]
    block[2 * TOK :, :] = span_lines(span_ref, KBLOCK - 2 * TOK).astype(BF)
    copies = [pltpu.make_async_copy(block, out_ref.at[w], sem.at[w]) for w in range(out_ref.shape[0])]
    for copy in copies:
        copy.start()
    for copy in copies:
        copy.wait()


def prep_kernel(span_ref, q_ref, g_ref, o_ref, lse_ref, out_ref, kept_ref):
    lse_rows, delta_rows = [], []
    for s in range(2):
        rows = slice(s * SPAN, (s + 1) * SPAN)
        for pair in range(HQ // 2):
            prods = []
            for h in (2 * pair, 2 * pair + 1):
                cols = slice(h * HD, (h + 1) * HD)
                at = s * QROWS + h * SPAN
                g = g_ref[rows, cols]
                out_ref[at : at + SPAN, :] = q_ref[rows, cols]
                out_ref[HQ * TOK + at : HQ * TOK + at + SPAN, :] = g
                prods.append(g.astype(F32) * o_ref[rows, cols].astype(F32))
            both = jnp.concatenate(prods, axis=0)
            delta_rows.append(jnp.sum(both.T, axis=0, keepdims=True))
            lse_rows.append(
                jnp.concatenate(
                    [lse_ref[2 * pair : 2 * pair + 1, rows], lse_ref[2 * pair + 1 : 2 * pair + 2, rows]],
                    axis=1,
                )
            )
    parts = []
    for rows in (lse_rows, delta_rows):
        rest = jnp.concatenate(rows, axis=0)
        for _ in range(3):
            piece = rest.astype(BF).astype(F32)
            rest = rest - piece
            parts.append(piece)
    parts.append(span_lines(span_ref, 8))
    out_ref[2 * HQ * TOK :, :] = jnp.concatenate(parts, axis=0).astype(BF)
    kept_ref[...] = jnp.concatenate(parts[:6], axis=0)


def plan_tiles(span_ref, other_blocks, gkv_ref, boundary):
    spans_q, spans_k = 2 * len(other_blocks) + 2, 2 * gkv_ref.shape[0]
    lines = max(spans_q, spans_k, 16)
    sub = lax.broadcasted_iota(jnp.int32, (lines, HD), 0)
    lane = lax.broadcasted_iota(jnp.int32, (lines, HD), 1)

    def column(tags):
        out = jnp.full((lines, HD), -1.0, F32)
        for b, tag in enumerate(tags):
            tag = tag.astype(F32)
            out = jnp.where(sub >> 1 == b, jnp.concatenate([tag] * (lines // tag.shape[0]), axis=0), out)
        return out.astype(jnp.int32)

    def total(rows):
        return jnp.sum(rows, axis=0, keepdims=True)

    k = column([gkv_ref[w, 2 * TOK : 2 * TOK + 16, :] for w in range(spans_k // 2)])
    q = column([span_lines(span_ref, 8)] + [block[2 * HQ * TOK + 16 : 2 * HQ * TOK + 32, :][8:] for block in other_blocks])
    first = jnp.where(q * SPAN >= boundary, boundary >> 6, 0)
    zero = jnp.zeros((lines, HD), jnp.int32)
    rank, below, upto = zero, zero, zero
    for j in range(spans_k):
        one = k[j : j + 1]
        rank = rank + (one < k).astype(jnp.int32)
        below = below + (one < first).astype(jnp.int32)
        upto = upto + (one <= q).astype(jnp.int32)
    real_k = sub < spans_k
    rank_line = total(jnp.where((lane == sub) & real_k, rank, 0))
    in_order = total(jnp.where((lane == rank) & real_k, k, 0)) + jnp.where(lane[:1] >= spans_k, 1 << 20, 0)
    count = jnp.where(sub < spans_q, (upto - below + PER - 1) >> (PER.bit_length() - 1), 0)
    end = zero
    for i in range(spans_q):
        end = end + jnp.where(sub >= i, count[i : i + 1], 0)
    place = total(jnp.where((lane >= end) & (sub < spans_q), 1, 0))
    mine = sub == place
    chunk = total(jnp.where(mine, below + PER * (count - end), 0)) + PER * lane[:1]
    span = total(jnp.where(mine, q, 0))
    unused = place >= spans_q
    span = jnp.where(unused, -(1 << 20), span)
    chunk = jnp.where(unused, 0, chunk)
    place = jnp.where(unused, 0, place)
    n_tiles = end[spans_q - 1 : spans_q]
    return jnp.concatenate([rank_line, in_order, span, place, chunk, n_tiles, n_tiles, n_tiles], axis=0)


def tile_kernel(n_q, n_x, n_k, doc_ref, span_ref, *refs):
    (own_q, own_g, own_rows), other_blocks, gkv_ref, refs = refs[:3], refs[3 : n_q + 2], refs[n_q + 2], refs[n_q + 3 :]
    dq_refs, dkv_out, refs = refs[:n_x], refs[n_x], refs[n_x + 1 :]
    dkv_ref, plan_v, plan_s, sems, q_s, g_s, k_s, v_s, dk_acc, dv_acc, dqt_acc, lse_s, del_s = refs
    spans_k = 2 * n_k
    scale = 1.0 / math.sqrt(HD)
    log2e = 1.0 / math.log(2.0)
    boundary = doc_ref[0]

    plan_v[...] = plan_tiles(span_ref, other_blocks, gkv_ref, boundary)
    tell = pltpu.make_async_copy(plan_v, plan_s, sems.at[0])
    tell.start()
    k_s[spans_k * SPAN :, :] = jnp.zeros((CHUNK - SPAN, HD), BF)
    v_s[spans_k * SPAN :, :] = jnp.zeros((CHUNK - SPAN, HD), BF)
    dk_acc[...] = jnp.zeros_like(dk_acc)
    dv_acc[...] = jnp.zeros_like(dv_acc)
    dqt_acc[...] = jnp.zeros_like(dqt_acc)
    for s in range(2):
        for h in range(HQ):
            at = s * QROWS + h * SPAN
            rows, cols = slice(s * SPAN, (s + 1) * SPAN), slice(h * HD, (h + 1) * HD)
            q_s[at : at + SPAN, :] = own_q[rows, cols]
            g_s[at : at + SPAN, :] = own_g[rows, cols]
    for b in range(n_q):
        if b == 0:
            extra = own_rows[...]
        else:
            block = other_blocks[b - 1]
            q_s[b * 2 * QROWS : (b + 1) * 2 * QROWS, :] = block[: HQ * TOK, :]
            g_s[b * 2 * QROWS : (b + 1) * 2 * QROWS, :] = block[HQ * TOK : 2 * HQ * TOK, :]
            extra = block[2 * HQ * TOK : 2 * HQ * TOK + 24, :].astype(F32)
        lse = (extra[0:4] + extra[4:8] + extra[8:12]) * log2e
        dlt = extra[12:16] + extra[16:20] + extra[20:24]
        for s in range(2):
            i = 2 * b + s
            lse_s[i] = jnp.broadcast_to(jnp.concatenate([lse[2 * s : 2 * s + 1], lse[2 * s + 1 : 2 * s + 2]], axis=1), (8, QROWS))
            del_s[i] = jnp.broadcast_to(jnp.concatenate([dlt[2 * s : 2 * s + 1], dlt[2 * s + 1 : 2 * s + 2]], axis=1), (8, QROWS))
    tell.wait()
    n_tiles = plan_s[5, 0]
    for w in range(n_k):
        for s in range(2):
            to = pl.ds(pl.multiple_of(plan_s[0, 2 * w + s] * SPAN, SPAN), SPAN)
            k_s[to, :] = gkv_ref[w, s * SPAN : (s + 1) * SPAN, :]
            v_s[to, :] = gkv_ref[w, TOK + s * SPAN : TOK + (s + 1) * SPAN, :]

    key_line = lax.broadcasted_iota(jnp.int32, (SPAN, QROWS), 0)
    row_off = lax.broadcasted_iota(jnp.int32, (1, QROWS), 1) % SPAN

    def open_tile(t):
        span, i, c = plan_s[2, t], plan_s[3, t], plan_s[4, t]
        q_rows = pl.ds(pl.multiple_of(i * QROWS, QROWS), QROWS)
        k_rows = pl.ds(pl.multiple_of(c * SPAN, SPAN), CHUNK)
        score = nt(k_s[k_rows, :], q_s[q_rows, :])
        dprob = nt(v_s[k_rows, :], g_s[q_rows, :])
        lse, dlt = lse_s[i][0:1], del_s[i][0:1]
        q_pos = span * SPAN + row_off
        q_start = jnp.where(q_pos >= boundary, boundary, 0)
        probs, dscores = [], []
        for j in range(PER):
            part = slice(j * SPAN, (j + 1) * SPAN)
            base = plan_s[1, c + j] * SPAN
            live = (key_line <= q_pos - base) & (key_line >= q_start - base)
            prob = jnp.where(live, jnp.exp2(score[part] * (scale * log2e) - lse), 0.0)
            probs.append(prob.astype(BF))
            dscores.append((prob * (dprob[part] - dlt)).astype(BF))
        return i, c, q_rows, k_rows, jnp.concatenate(probs, axis=0), jnp.concatenate(dscores, axis=0)

    def close_tile(i, c, q_rows, k_rows, prob_b, dscore_b):
        dv_acc[k_rows, :] += nn(prob_b, g_s[q_rows, :])
        dk_acc[k_rows, :] += nn(dscore_b, q_s[q_rows, :])
        dqt_acc[i] += tn(dscore_b, k_s[k_rows, :])

    def step(t, _):
        for u in range(0, UNROLL, 2):
            for opened in [open_tile(UNROLL * t + u), open_tile(UNROLL * t + u + 1)]:
                close_tile(*opened)
        return 0

    lax.fori_loop(0, (n_tiles + UNROLL - 1) // UNROLL, step, 0)
    sends = []
    for w in range(n_k):
        for s in range(2):
            at = pl.ds(pl.multiple_of(plan_s[0, 2 * w + s] * SPAN, SPAN), SPAN)
            dkv_ref[w, s * SPAN : (s + 1) * SPAN, :] = dk_acc[at, :].astype(BF)
            dkv_ref[w, TOK + s * SPAN : TOK + (s + 1) * SPAN, :] = dv_acc[at, :].astype(BF)
        if w % 4 == 3:
            some = pl.ds(w - 3, 4)
            sends.append(pltpu.make_async_copy(dkv_ref.at[some], dkv_out.at[some], sems.at[1 + w // 4]))
            sends[-1].start()
    for i in range(2 * n_q):
        dq = (dqt_acc[i] * scale).astype(BF)
        place, s = i // 2, i % 2
        at = place // n_x * TOK + s * SPAN
        for h in range(HQ):
            dq_refs[place % n_x][at : at + SPAN, h * HD : (h + 1) * HD] = dq[h * SPAN : (h + 1) * SPAN]
    for send in sends:
        send.wait()


def tile_grads(doc_lengths, span_order, own, q_blocks, gkv, n_x):
    n_q, n_k = len(q_blocks) + 1, gkv.shape[0]
    keys, rows = n_k * TOK, 2 * n_q * QROWS
    outs = pl.pallas_call(
        lambda *refs: tile_kernel(n_q, n_x, n_k, *refs),
        out_shape=[jax.ShapeDtypeStruct((n_q // n_x * TOK, HQ * HD), BF)] * n_x + [jax.ShapeDtypeStruct((n_k, 2 * TOK, HD), BF)],
        in_specs=[SMEM, SMEM] + [VMEM] * (n_q + 3),
        out_specs=[VMEM] * n_x + [pl.BlockSpec(memory_space=pl.ANY)],
        scratch_shapes=[
            pltpu.VMEM((n_k, 2 * TOK, HD), BF),
            pltpu.VMEM((8, HD), jnp.int32),
            pltpu.SMEM((8, HD), jnp.int32),
            pltpu.SemaphoreType.DMA((1 + n_k // 4,)),
            pltpu.VMEM((rows, HD), BF),
            pltpu.VMEM((rows, HD), BF),
            pltpu.VMEM((keys + CHUNK - SPAN, HD), BF),
            pltpu.VMEM((keys + CHUNK - SPAN, HD), BF),
            pltpu.VMEM((keys + CHUNK - SPAN, HD), F32),
            pltpu.VMEM((keys + CHUNK - SPAN, HD), F32),
            pltpu.VMEM((2 * n_q, QROWS, HD), F32),
            pltpu.VMEM((2 * n_q, 8, QROWS), F32),
            pltpu.VMEM((2 * n_q, 8, QROWS), F32),
        ],
        compiler_params=pltpu.CompilerParams(vmem_limit_bytes=32 * 1024 * 1024),
        cost_estimate=pl.CostEstimate(flops=5_000_000_000, bytes_accessed=4_000_000, transcendentals=2_000_000),
        name="tile_grads",
    )(doc_lengths, span_order, *own, *q_blocks, gkv)
    return outs[:n_x], outs[n_x]


def partial_kernel(own_ref, other_ref, swapped_ref, out_ref):
    cols = out_ref.shape[2]
    for h in range(out_ref.shape[0]):
        at = slice(h * cols, (h + 1) * cols)
        out_ref[h] = (own_ref[:, at] + nt(other_ref[...], swapped_ref[at, :])).astype(BF)


def partial_hidden(own, other, swapped, n_hi):
    return pl.pallas_call(
        partial_kernel,
        out_shape=jax.ShapeDtypeStruct((n_hi, own.shape[0], own.shape[1] // n_hi), BF),
        in_specs=[VMEM] * 3,
        out_specs=VMEM,
        compiler_params=pltpu.CompilerParams(vmem_limit_bytes=16 * 1024 * 1024),
        name="partial_hidden",
    )(own, other, swapped)


def prep(span_order, queries, grad_out, fwd_out, log_norm):
    return pl.pallas_call(
        prep_kernel,
        out_shape=[jax.ShapeDtypeStruct((QBLOCK, HD), BF), jax.ShapeDtypeStruct((24, HD), F32)],
        in_specs=[SMEM, VMEM, VMEM, VMEM, VMEM],
        out_specs=[VMEM] * 2,
        name="prep",
    )(span_order, queries, grad_out, fwd_out, log_norm)


def pack(span_order, key_rows, value_rows, copies):
    return pl.pallas_call(
        pack_kernel,
        out_shape=jax.ShapeDtypeStruct((copies, KBLOCK, HD), BF),
        in_specs=[SMEM, VMEM, VMEM],
        out_specs=pl.BlockSpec(memory_space=pl.ANY),
        scratch_shapes=[pltpu.VMEM((KBLOCK, HD), BF), pltpu.SemaphoreType.DMA((copies,))],
        name="pack",
    )(span_order, key_rows, value_rows)


def hop(block, axis, shift):
    n = lax.axis_size(axis)
    return lax.ppermute(block, axis, [(i, (i + shift) % n) for i in range(n)])


def body(queries, key_rows, value_rows, grad_out, fwd_out, log_norm, span_order, doc_lengths, key_proj, value_proj):
    n_q, n_k = lax.axis_size("x"), lax.axis_size(KEYS)
    n_hi = lax.axis_size("y_hi")
    core = lax.axis_index("core")

    gkv = lax.all_to_all(pack(span_order, key_rows, value_rows, n_k), KEYS, 0, 0)
    mine, own_rows = prep(span_order, queries, grad_out, fwd_out, log_norm)
    q_blocks = [hop(mine, "x", shift) for shift in range(1, n_q)]

    cols = key_proj.shape[0] // (2 * n_hi)
    projs = jnp.concatenate([key_proj, value_proj], axis=1).reshape(n_hi, 2, cols, 2 * HD)
    kept = lax.dynamic_index_in_dim(projs, core, 1, keepdims=False).reshape(n_hi * cols, 2 * HD)
    given = lax.dynamic_index_in_dim(projs, 1 - core, 1, keepdims=False).reshape(n_hi * cols, 2 * HD)
    swapped = hop(given, "core", 1)

    dqs, dkv = tile_grads(doc_lengths, span_order, (queries, grad_out, own_rows), q_blocks, gkv, n_q)

    parts = lax.all_to_all(dkv, KEYS, 0, 0)
    homes = [dqs[0]] + [hop(dqs[shift], "x", -shift) for shift in range(1, n_q)]
    parts, homes, swapped = lax.optimization_barrier((parts, homes, swapped))
    grad_query = sum(h.astype(F32) for h in homes).astype(BF)
    total = jnp.sum(parts.astype(F32), axis=0)
    grad_key = (total[:TOK] * (1.0 / math.sqrt(HD))).astype(BF)
    grad_value = total[TOK:].astype(BF)
    both = jnp.concatenate([grad_key, grad_value], axis=1)

    partial = partial_hidden(nt(both, kept), hop(both, "core", 1), swapped, n_hi)
    shares = lax.all_to_all(partial, "y_hi", 0, 0)
    hidden = jnp.sum(shares.astype(F32), axis=0).astype(BF)
    return grad_query, grad_key, grad_value, hidden


def solution(mesh):
    fine = Mesh(mesh.devices.reshape(4, 2, 8, 4, 2), AXES)
    placed = (
        P(CTX, KV),
        P(CTX, KV),
        P(CTX, KV),
        P(CTX, KV),
        P(CTX, KV),
        P(KV, CTX),
        P(CTX),
        P(),
        P(None, KV),
        P(None, KV),
    )
    return jax.shard_map(
        body,
        mesh=fine,
        in_specs=placed,
        out_specs=(P(CTX, KV), P(CTX, KV), P(CTX, KV), P(CTX, KV)),
        check_vma=False,
    )
```
